256 devices in a mesh: rows: 32 (over z, x), cols: 8 (over y, core).
Axes of the slice: x: 4, y: 4, z: 8, core: 2. Of those that a mesh axis runs over, the one named last changes fastest.
Arguments:
- points: float32 [16, 262144], P(None, ('rows', 'cols')), may hold values from -6 to 6
- lengthscales: float32 [16], replicated, may hold values from 2 to 3
- targets: float32 [64, 262144], P(None, ('rows', 'cols')), may hold values from -6 to 6
- inducing_weights: bfloat16 [64, 2048], P(None, 'cols'), may hold values from -0.59765625 to 0.59765625
- inducing_index: int32 [2048], replicated, may hold values from 0 to 262143
- block_order: int32 [3], replicated, may hold values from 0 to 255
- block_inverse: bfloat16 [256, 1024, 1024], P(('rows', 'cols')), may hold values from -0.1 to 0.1
Outputs:
- residual: float32 [64, 262144], P(None, ('rows', 'cols'))
- weights: float32 [64, 262144], P(None, ('rows', 'cols'))
The draws below stay inside these ranges and needn't reach their ends.
All inputs are finite; a program needn't handle non-finite values.
Results may differ from the reference program's by a relative error of at most 0.00095.
The reference program's roundings to bfloat16 on the way count: a program that leaves them out, or rounds other values in their place, can miss the bound.
Values may be sent and summed in bfloat16 or wider, within the bound.
A program may use at most 64 MiB of HBM per device.

```python
import math
import jax
import jax.numpy as jnp
from jax import lax

DIM = 16
COLS = 64
INDUCING = 2048
BLK = 1024
PTS_DEV = 1024
STEPS = 3
NPTS = 262144
BLOCKS = 256


def draw_points(key, part):
    point_key = jax.random.fold_in(key, 29)
    values = jnp.clip(1.5 * jax.random.normal(point_key, (DIM, NPTS), jnp.float32), -6.0, 6.0)
    return values


def draw_block_inverse(key, part):
    first_key, second_key = jax.random.split(jax.random.fold_in(key, 17))
    diagonal = jnp.exp(jax.random.uniform(first_key, (BLOCKS, BLK), jnp.float32, math.log(0.03), math.log(0.099)))
    offdiag = jnp.clip(jax.random.normal(second_key, (BLOCKS, BLK, BLK), jnp.float32), -4.0, 4.0)
    offdiag = offdiag * (0.012 / math.sqrt(BLK))
    identity = jnp.eye(BLK, dtype=jnp.float32)
    return (offdiag * (1.0 - identity) + diagonal[:, :, None] * identity).astype(jnp.bfloat16)


def place_ends(array, key, least, largest):
    longest = array.shape.index(max(array.shape))
    spots = []
    for shift in (0, 1):
        where = [jax.random.randint(jax.random.fold_in(key, axis), (), 0, length) for axis, length in enumerate(array.shape)]
        where[longest] = (where[longest] + shift) % array.shape[longest]
        spots.append(tuple(where))
    return array.at[spots[0]].set(least).at[spots[1]].set(largest)


def levels(rng, dims, shards, smallest, largest):
    def one(dim, blocks):
        steps = jax.random.uniform(jax.random.fold_in(jax.random.fold_in(rng, 6), dim), (blocks,), jnp.float32, smallest / len(shards), largest / len(shards))
        return jnp.repeat(jnp.exp(steps), dims[dim] // blocks).reshape((-1,) + (1,) * (len(dims) - dim - 1))

    factor_of = one(*shards[0])
    for cut in shards[1:]:
        factor_of = factor_of * one(*cut)
    return factor_of


def bell_draw(own_key, extent, spread, bound, shards=(), held_as=jnp.bfloat16):
    entries = spread * jax.random.normal(own_key, extent, jnp.float32)
    if shards:
        entries = entries * levels(own_key, extent, shards, -0.22, 0.18)
    return jnp.clip(entries, -bound, bound).astype(held_as)


def setup_inputs(seed: int = 0) -> dict:
    splits = jax.random.split(jax.random.key(seed), 8)
    points = draw_points(jax.random.fold_in(splits[7], 71), 0)
    lengthscales = jnp.clip(jnp.exp(jax.random.uniform(splits[1], (DIM,), jnp.float32, math.log(2.0), math.log(3.0))), 2.0, 3.0)
    targets = bell_draw(splits[2], (COLS, NPTS), 1.0, 6.0, ((1, 256),), jnp.float32)
    inducing_weights = bell_draw(splits[3], (COLS, INDUCING), 0.1, 0.59765625, ((1, 8),))
    inducing_index = place_ends(jax.random.randint(splits[4], (INDUCING,), 0, NPTS), jax.random.fold_in(splits[4], 1), 0, NPTS - 1).astype(jnp.int32)
    block_order = jax.random.randint(splits[5], (STEPS,), 0, BLOCKS).astype(jnp.int32)
    block_inverse = draw_block_inverse(jax.random.fold_in(splits[7], 71), 0)
    return {"points": points, "lengthscales": lengthscales, "targets": targets, "inducing_weights": inducing_weights, "inducing_index": inducing_index, "block_order": block_order, "block_inverse": block_inverse}


noise_var = 0.5


def kernel_tile(left, right):
    crossed = lax.dot_general(left, right, (((0,), (0,)), ((), ())), precision=lax.Precision.HIGHEST, preferred_element_type=jnp.float32)
    left_sq = jnp.sum(left * left, axis=0)
    right_sq = jnp.sum(right * right, axis=0)
    return jnp.exp(-0.5 * (left_sq[:, None] + right_sq[None, :] - 2.0 * crossed)).astype(jnp.bfloat16)


def reference(points, lengthscales, targets, inducing_weights, inducing_index, block_order, block_inverse):
    scaled = points / lengthscales[:, None]
    anchors = jnp.take(scaled, inducing_index, axis=1)
    slab_count = NPTS // PTS_DEV

    def warm_slab(slab_no):
        coords = lax.dynamic_slice_in_dim(scaled, slab_no * PTS_DEV, PTS_DEV, 1)
        return jnp.dot(inducing_weights, kernel_tile(anchors, coords), preferred_element_type=jnp.float32)

    predicted = lax.map(warm_slab, jnp.arange(slab_count, dtype=jnp.int32))
    predicted = jnp.transpose(predicted, (1, 0, 2)).reshape(COLS, NPTS)
    residual = targets - predicted
    weights = jnp.zeros((COLS, NPTS), jnp.float32)
    for step_no in range(STEPS):
        block_id = block_order[step_no]
        offset = (block_id * BLK).astype(jnp.int32)
        shifted = lax.dynamic_slice_in_dim(residual, offset, BLK, 1).astype(jnp.bfloat16)
        delta = jnp.dot(shifted, block_inverse[block_id], preferred_element_type=jnp.float32).astype(jnp.bfloat16)
        block_coords = lax.dynamic_slice_in_dim(scaled, offset, BLK, 1)

        def step_slab(slab_no):
            coords = lax.dynamic_slice_in_dim(scaled, slab_no * PTS_DEV, PTS_DEV, 1)
            return jnp.dot(delta, kernel_tile(block_coords, coords), preferred_element_type=jnp.float32)

        updates = lax.map(step_slab, jnp.arange(slab_count, dtype=jnp.int32))
        residual = residual - jnp.transpose(updates, (1, 0, 2)).reshape(COLS, NPTS)
        delta_f = delta.astype(jnp.float32)
        block_res = lax.dynamic_slice_in_dim(residual, offset, BLK, 1)
        residual = lax.dynamic_update_slice_in_dim(residual, block_res - noise_var * delta_f, offset, 1)
        block_wts = lax.dynamic_slice_in_dim(weights, offset, BLK, 1)
        weights = lax.dynamic_update_slice_in_dim(weights, block_wts + delta_f, offset, 1)
    return residual, weights
```

```python
import functools
import math

import jax
import jax.numpy as jnp
from jax import lax
from jax.experimental import pallas as pl
from jax.experimental.pallas import tpu as pltpu
from jax.sharding import PartitionSpec as P

MESH = pl.DeviceIdType.MESH
noise_var = 0.5
LOG2E = math.log2(math.e)

DIM = 16
COLS = 64
PTS = 1024
STEPS = 3
PLANES = 8
GROUP = 32
INDUCING = 2048
LANES = 128


def split3(x):
    high = x.astype(jnp.bfloat16)
    rest = x - high.astype(jnp.float32)
    mid = rest.astype(jnp.bfloat16)
    low = (rest - mid.astype(jnp.float32)).astype(jnp.bfloat16)
    return high, mid, low


def norm_rows(norm, first):
    parts = [p.astype(jnp.float32) for p in split3(norm)]
    row = lax.broadcasted_iota(jnp.int32, (16, norm.shape[1]), 0)
    one_from = 3 - first
    out = jnp.where((row >= one_from) & (row < one_from + 3), 1.0, 0.0)
    for k in range(3):
        out = jnp.where(row == first + k, parts[k], out)
    return out.astype(jnp.bfloat16)


def left_rows(high, mid, low, x):
    norm = (-0.5 * LOG2E) * jnp.sum(x * x, axis=0, keepdims=True)
    rows = norm_rows(norm, 0)
    return jnp.concatenate([high, high, mid, high, low, mid, rows, jnp.zeros_like(rows)], axis=0)


def right_rows(x):
    norm = (-0.5 * LOG2E) * jnp.sum(x * x, axis=0, keepdims=True)
    high, mid, low = split3(x * LOG2E)
    rows = norm_rows(norm, 3)
    return jnp.concatenate([high, mid, high, low, high, mid, rows, jnp.zeros_like(rows)], axis=0)


def tile_of(left, right):
    power = lax.dot_general(
        left, right, (((0,), (0,)), ((), ())), preferred_element_type=jnp.float32
    )
    return jnp.exp2(power).astype(jnp.bfloat16)


def body(
    pts_ref,
    scale_ref,
    targets_ref,
    own_w_ref,
    index_ref,
    order_ref,
    inverse_ref,
    res_ref,
    wts_ref,
    inverse,
    w_all,
    right,
    a_send,
    a_recv,
    a_mid,
    a_all,
    x_send,
    x_recv,
    x_mid,
    x_all,
    cand,
    d_recv0,
    d_recv1,
    d_recv2,
    d_mid0,
    d_mid1,
    d_mid2,
    d_all,
    ktile,
    local_sem,
    send_sem,
    recv_sem,
):
    d_recv = (d_recv0, d_recv1, d_recv2)
    d_mid = (d_mid0, d_mid1, d_mid2)
    row_id = lax.axis_index("rows")
    col_id = lax.axis_index("cols")
    z = row_id // 4
    spot = (row_id % 4) * 8 + col_id
    me = row_id * 8 + col_id

    def device(plane, place):
        return (plane * 4 + place // 8, place % 8)

    barrier = pltpu.get_barrier_semaphore()

    @pl.loop(1, GROUP)
    def _(k):
        pl.semaphore_signal(
            barrier, inc=1, device_id=device(z, (spot + k) % GROUP), device_id_type=MESH
        )

    @pl.loop(1, PLANES)
    def _(k):
        pl.semaphore_signal(
            barrier, inc=1, device_id=device((z + k) % PLANES, spot), device_id_type=MESH
        )

    get_inverse = pltpu.make_async_copy(inverse_ref.at[0], inverse, local_sem.at[0])
    get_targets = pltpu.make_async_copy(targets_ref, res_ref, local_sem.at[1])
    get_w = pltpu.make_async_copy(own_w_ref, w_all.at[col_id], local_sem.at[2])
    get_w.start()
    get_targets.start()
    get_inverse.start()

    pending = []

    def scatter(phase, src, dst):
        @pl.loop(1, GROUP)
        def _(k):
            place = (spot + k) % GROUP
            pltpu.make_async_remote_copy(
                src_ref=src.at[place],
                dst_ref=dst.at[spot],
                send_sem=send_sem.at[phase],
                recv_sem=recv_sem.at[phase],
                device_id=device(z, place),
                device_id_type=MESH,
            ).start()

        dst[spot] = src[spot]
        return arrival(phase, dst, GROUP - 1, device(z, (spot + 1) % GROUP))

    def arrival(phase, dst, count, other):
        some = dst.at[pl.ds(0, count)]
        all_of_them = pltpu.make_async_remote_copy(
            src_ref=some,
            dst_ref=some,
            send_sem=send_sem.at[phase],
            recv_sem=recv_sem.at[phase],
            device_id=other,
            device_id_type=MESH,
        )
        pending.append(all_of_them)
        return all_of_them

    def along_z(phase, dst):
        @pl.loop(1, PLANES)
        def _(k):
            pltpu.make_async_remote_copy(
                src_ref=dst.at[z],
                dst_ref=dst.at[z],
                send_sem=send_sem.at[phase],
                recv_sem=recv_sem.at[phase],
                device_id=device((z + k) % PLANES, spot),
                device_id_type=MESH,
            ).start()

        return arrival(phase, dst, PLANES - 1, device((z + 1) % PLANES, spot))

    def in_plane(phase, dst):
        @pl.loop(1, GROUP)
        def _(k):
            pltpu.make_async_remote_copy(
                src_ref=dst.at[spot],
                dst_ref=dst.at[spot],
                send_sem=send_sem.at[phase],
                recv_sem=recv_sem.at[phase],
                device_id=device(z, (spot + k) % GROUP),
                device_id_type=MESH,
            ).start()

        return arrival(phase, dst, GROUP - 1, device(z, (spot + 1) % GROUP))

    feature = lax.broadcasted_iota(jnp.int32, (DIM, PTS), 0)
    scales = jnp.zeros((DIM, PTS), jnp.float32)
    for k in range(DIM):
        scales = jnp.where(feature == k, scale_ref[k], scales)
    scaled = pts_ref[...] / scales
    right[...] = right_rows(scaled)
    parts = split3(scaled)
    for p in range(3):
        for g in range(8):
            x_send[p * 8 + g] = parts[p][:, g * LANES : (g + 1) * LANES]
    x_send[pl.ds(24, 8)] = jnp.zeros((8, 16, LANES), jnp.bfloat16)
    stacked = jnp.concatenate(
        [parts[p][:, g * LANES : (g + 1) * LANES] for g in range(8) for p in range(3)], axis=0
    )
    lane_row = lax.broadcasted_iota(jnp.int32, (LANES, LANES), 0)
    local = index_ref[...] - me * PTS
    inside = (local >= 0) & (local < PTS)
    group_of = jnp.where(inside, local >> 7, -1)
    lane_of = local & (LANES - 1)
    for j in range(INDUCING // LANES):
        one_hot = jnp.where(lane_row == lane_of[j : j + 1], 1.0, 0.0).astype(jnp.bfloat16)
        picked = jnp.dot(stacked, one_hot, preferred_element_type=jnp.float32)
        which = jnp.broadcast_to(group_of[j : j + 1], (48, LANES))
        kept = jnp.zeros((48, LANES), jnp.float32)
        for g in range(8):
            kept = jnp.where(which == g, picked[g * 48 : (g + 1) * 48], kept)
        coords = kept[0:16] + kept[16:32] + kept[32:48]
        a_send[j] = coords[0:8]
        a_send[16 + j] = coords[8:16]

    pl.semaphore_wait(barrier, GROUP - 1 + PLANES - 1)

    a1 = scatter(0, a_send, a_recv)
    x1 = scatter(1, x_send, x_recv)
    get_w.wait()

    @pl.loop(1, 8)
    def _(k):
        pltpu.make_async_remote_copy(
            src_ref=w_all.at[col_id],
            dst_ref=w_all.at[col_id],
            send_sem=send_sem.at[2],
            recv_sem=recv_sem.at[2],
            device_id=(row_id, (col_id + k) % 8),
            device_id_type=MESH,
        ).start()

    w1 = arrival(2, w_all, 7, (row_id, (col_id + 1) % 8))

    owners = [order_ref[s] for s in range(STEPS)]
    owner_spot = [o & (GROUP - 1) for o in owners]
    owner_z = [o >> 5 for o in owners]

    a1.wait_recv()
    a_mid[z] = jnp.sum(a_recv[...], axis=0)
    a2 = along_z(3, a_mid)
    x1.wait_recv()
    for s in range(STEPS):
        x_mid[z, s] = x_recv[owner_spot[s]]
    x2 = along_z(4, x_mid)
    a2.wait_recv()
    a_all[spot] = jnp.sum(a_mid[...], axis=0)
    a3 = in_plane(5, a_all)
    x2.wait_recv()
    for s in range(STEPS):
        x_all[spot, s] = x_mid[owner_z[s], s]
    a3.wait_recv()
    x3 = in_plane(6, x_all)

    w1.wait_recv()
    get_targets.wait()

    @pl.loop(0, INDUCING // 256)
    def _(i):
        coords = jnp.concatenate(
            [
                jnp.concatenate([a_all[2 * i], a_all[2 * i + 1]], axis=1),
                jnp.concatenate([a_all[16 + 2 * i], a_all[16 + 2 * i + 1]], axis=1),
            ],
            axis=0,
        )
        left = left_rows(*split3(coords), coords)
        res_ref[...] -= jnp.dot(
            w_all[i], tile_of(left, right[...]), preferred_element_type=jnp.float32
        )

    wts_ref[...] = jnp.zeros_like(wts_ref)
    get_inverse.wait()

    def block_tile(s):
        @pl.loop(0, 4)
        def _(i):
            planes = [
                jnp.concatenate(
                    [x_all[p * 8 + 2 * i, s], x_all[p * 8 + 2 * i + 1, s]], axis=1
                )
                for p in range(3)
            ]
            coords = sum(p.astype(jnp.float32) for p in planes)
            left = left_rows(*planes, coords)
            ktile[s, pl.ds(pl.multiple_of(i * 256, 256), 256), :] = tile_of(left, right[...])

    for s in range(STEPS):
        shifted = res_ref[...].astype(jnp.bfloat16)
        for g in range(4):
            part = jnp.dot(
                shifted,
                inverse[:, g * 256 : (g + 1) * 256],
                preferred_element_type=jnp.float32,
            ).astype(jnp.bfloat16)
            for r in range(4):
                for h in range(2):
                    cand[s, r * 8 + g * 2 + h] = part[
                        r * 16 : (r + 1) * 16, h * LANES : (h + 1) * LANES
                    ]
        d1 = scatter(7 + 3 * s, cand.at[s], d_recv[s])
        if s == 0:
            x3.wait_recv()
            block_tile(0)
        d1.wait_recv()
        d_mid[s][z] = d_recv[s][owner_spot[s]]
        d2 = along_z(8 + 3 * s, d_mid[s])
        if s < STEPS - 1:
            block_tile(s + 1)
        d2.wait_recv()
        d_all[s, spot] = d_mid[s][owner_z[s]]
        d3 = in_plane(9 + 3 * s, d_all.at[s])
        d3.wait_recv()
        delta = jnp.concatenate(
            [
                jnp.concatenate([d_all[s, r * 8 + g] for g in range(8)], axis=1)
                for r in range(4)
            ],
            axis=0,
        )
        mine = (owners[s] == me).astype(jnp.float32)
        delta_f = delta.astype(jnp.float32) * mine
        update = jnp.dot(delta, ktile[s], preferred_element_type=jnp.float32)
        res_ref[...] = (res_ref[...] - update) - noise_var * delta_f
        wts_ref[...] += delta_f

    for transfer in pending:
        transfer.wait_send()


def projected(points, lengthscales, targets, inducing_weights, inducing_index, block_order, block_inverse):
    vmem = pl.BlockSpec(memory_space=pltpu.VMEM)
    smem = pl.BlockSpec(memory_space=pltpu.SMEM)
    anywhere = pl.BlockSpec(memory_space=pl.ANY)
    out = jax.ShapeDtypeStruct((COLS, PTS), jnp.float32)
    bf16, f32 = jnp.bfloat16, jnp.float32
    return pl.pallas_call(
        body,
        out_shape=(out, out),
        in_specs=[vmem, smem, anywhere, anywhere, vmem, smem, anywhere],
        out_specs=(vmem, vmem),
        scratch_shapes=[
            pltpu.VMEM((PTS, PTS), bf16),
            pltpu.VMEM((8, COLS, 256), bf16),
            pltpu.VMEM((LANES, PTS), bf16),
            pltpu.VMEM((GROUP, 8, LANES), f32),
            pltpu.VMEM((GROUP, 8, LANES), f32),
            pltpu.VMEM((PLANES, 8, LANES), f32),
            pltpu.VMEM((GROUP, 8, LANES), f32),
            pltpu.VMEM((GROUP, 16, LANES), bf16),
            pltpu.VMEM((GROUP, 16, LANES), bf16),
            pltpu.VMEM((PLANES, STEPS, 16, LANES), bf16),
            pltpu.VMEM((GROUP, STEPS, 16, LANES), bf16),
            pltpu.VMEM((STEPS, GROUP, 16, LANES), bf16),
            *[pltpu.VMEM((GROUP, 16, LANES), bf16)] * STEPS,
            *[pltpu.VMEM((PLANES, 16, LANES), bf16)] * STEPS,
            pltpu.VMEM((STEPS, GROUP, 16, LANES), bf16),
            pltpu.VMEM((STEPS, PTS, PTS), bf16),
            pltpu.SemaphoreType.DMA((3,)),
            pltpu.SemaphoreType.DMA((16,)),
            pltpu.SemaphoreType.DMA((16,)),
        ],
        compiler_params=pltpu.CompilerParams(
            collective_id=0, has_side_effects=True, vmem_limit_bytes=32 << 20
        ),
        name="projection",
    )(
        points,
        lengthscales,
        targets,
        inducing_weights,
        inducing_index.reshape(INDUCING // LANES, LANES),
        block_order,
        block_inverse,
    )


def solution(mesh):
    placed = (
        P(None, ("rows", "cols")),
        P(),
        P(None, ("rows", "cols")),
        P(None, "cols"),
        P(),
        P(),
        P(("rows", "cols"), None, None),
    )
    return jax.shard_map(
        projected,
        mesh=mesh,
        in_specs=placed,
        out_specs=(P(None, ("rows", "cols")), P(None, ("rows", "cols"))),
        check_vma=False,
    )
```

```python
import functools
import math

import jax
import jax.numpy as jnp
from jax import lax
from jax.experimental import pallas as pl
from jax.experimental.pallas import tpu as pltpu
from jax.sharding import PartitionSpec as P

MESH = pl.DeviceIdType.MESH
noise_var = 0.5
LOG2E = math.log2(math.e)

DIM = 16
COLS = 64
PTS = 1024
STEPS = 3
PLANES = 8
GROUP = 32
INDUCING = 2048
LANES = 128


def split3(x):
    high = x.astype(jnp.bfloat16)
    rest = x - high.astype(jnp.float32)
    mid = rest.astype(jnp.bfloat16)
    low = (rest - mid.astype(jnp.float32)).astype(jnp.bfloat16)
    return high, mid, low


def norm_rows(norm, first):
    parts = [p.astype(jnp.float32) for p in split3(norm)]
    row = lax.broadcasted_iota(jnp.int32, (16, norm.shape[1]), 0)
    one_from = 3 - first
    out = jnp.where((row >= one_from) & (row < one_from + 3), 1.0, 0.0)
    for k in range(3):
        out = jnp.where(row == first + k, parts[k], out)
    return out.astype(jnp.bfloat16)


def left_rows(high, mid, low, x):
    norm = (-0.5 * LOG2E) * jnp.sum(x * x, axis=0, keepdims=True)
    rows = norm_rows(norm, 0)
    return jnp.concatenate([high, high, mid, high, low, mid, rows, jnp.zeros_like(rows)], axis=0)


def right_rows(x):
    norm = (-0.5 * LOG2E) * jnp.sum(x * x, axis=0, keepdims=True)
    high, mid, low = split3(x * LOG2E)
    rows = norm_rows(norm, 3)
    return jnp.concatenate([high, mid, high, low, high, mid, rows, jnp.zeros_like(rows)], axis=0)


def tile_of(left, right):
    power = lax.dot_general(
        left, right, (((0,), (0,)), ((), ())), preferred_element_type=jnp.float32
    )
    return jnp.exp2(power).astype(jnp.bfloat16)


def body(
    pts_hbm,
    scale_hbm,
    targets_ref,
    own_w_ref,
    index_hbm,
    order_hbm,
    inverse_ref,
    res_ref,
    wts_ref,
    pts_ref,
    scale_ref,
    index_ref,
    order_ref,
    inverse,
    w_all,
    right,
    a_send,
    a_recv,
    a_mid,
    a_all,
    x_send,
    x_recv,
    x_mid,
    x_all,
    cand,
    d_recv0,
    d_recv1,
    d_recv2,
    d_mid0,
    d_mid1,
    d_mid2,
    d_all,
    ktile,
    local_sem,
    send_sem,
    recv_sem,
):
    d_recv = (d_recv0, d_recv1, d_recv2)
    d_mid = (d_mid0, d_mid1, d_mid2)
    row_id = lax.axis_index("rows")
    col_id = lax.axis_index("cols")
    z = row_id // 4
    spot = (row_id % 4) * 8 + col_id
    me = row_id * 8 + col_id

    def device(plane, place):
        return (plane * 4 + place // 8, place % 8)

    barrier = pltpu.get_barrier_semaphore()

    @pl.loop(1, GROUP)
    def _(k):
        pl.semaphore_signal(
            barrier, inc=1, device_id=device(z, (spot + k) % GROUP), device_id_type=MESH
        )

    @pl.loop(1, PLANES)
    def _(k):
        pl.semaphore_signal(
            barrier, inc=1, device_id=device((z + k) % PLANES, spot), device_id_type=MESH
        )

    get_inverse = pltpu.make_async_copy(inverse_ref.at[0], inverse, local_sem.at[0])
    get_targets = pltpu.make_async_copy(targets_ref, res_ref, local_sem.at[1])
    get_w = pltpu.make_async_copy(own_w_ref, w_all.at[col_id], local_sem.at[2])
    small = [
        pltpu.make_async_copy(src, dst, local_sem.at[3 + k])
        for k, (src, dst) in enumerate(
            [
                (pts_hbm, pts_ref),
                (scale_hbm, scale_ref),
                (index_hbm, index_ref),
                (order_hbm, order_ref),
            ]
        )
    ]
    for copy in small:
        copy.start()
    get_w.start()
    get_targets.start()
    get_inverse.start()

    pending = []

    def scatter(phase, src, dst):
        @pl.loop(1, GROUP)
        def _(k):
            place = (spot + k) % GROUP
            pltpu.make_async_remote_copy(
                src_ref=src.at[place],
                dst_ref=dst.at[spot],
                send_sem=send_sem.at[phase],
                recv_sem=recv_sem.at[phase],
                device_id=device(z, place),
                device_id_type=MESH,
            ).start()

        dst[spot] = src[spot]
        return arrival(phase, dst, GROUP - 1, device(z, (spot + 1) % GROUP))

    def arrival(phase, dst, count, other):
        some = dst.at[pl.ds(0, count)]
        all_of_them = pltpu.make_async_remote_copy(
            src_ref=some,
            dst_ref=some,
            send_sem=send_sem.at[phase],
            recv_sem=recv_sem.at[phase],
            device_id=other,
            device_id_type=MESH,
        )
        pending.append(all_of_them)
        return all_of_them

    def along_z(phase, dst):
        @pl.loop(1, PLANES)
        def _(k):
            pltpu.make_async_remote_copy(
                src_ref=dst.at[z],
                dst_ref=dst.at[z],
                send_sem=send_sem.at[phase],
                recv_sem=recv_sem.at[phase],
                device_id=device((z + k) % PLANES, spot),
                device_id_type=MESH,
            ).start()

        return arrival(phase, dst, PLANES - 1, device((z + 1) % PLANES, spot))

    def in_plane(phase, dst):
        @pl.loop(1, GROUP)
        def _(k):
            pltpu.make_async_remote_copy(
                src_ref=dst.at[spot],
                dst_ref=dst.at[spot],
                send_sem=send_sem.at[phase],
                recv_sem=recv_sem.at[phase],
                device_id=device(z, (spot + k) % GROUP),
                device_id_type=MESH,
            ).start()

        return arrival(phase, dst, GROUP - 1, device(z, (spot + 1) % GROUP))

    for copy in small:
        copy.wait()
    feature = lax.broadcasted_iota(jnp.int32, (DIM, PTS), 0)
    scales = jnp.zeros((DIM, PTS), jnp.float32)
    for k in range(DIM):
        scales = jnp.where(feature == k, scale_ref[k], scales)
    scaled = pts_ref[...] / scales
    right[...] = right_rows(scaled)
    parts = split3(scaled)
    for p in range(3):
        for g in range(8):
            x_send[p * 8 + g] = parts[p][:, g * LANES : (g + 1) * LANES]
    x_send[pl.ds(24, 8)] = jnp.zeros((8, 16, LANES), jnp.bfloat16)
    stacked = jnp.concatenate(
        [parts[p][:, g * LANES : (g + 1) * LANES] for g in range(8) for p in range(3)], axis=0
    )
    lane_row = lax.broadcasted_iota(jnp.int32, (LANES, LANES), 0)
    local = index_ref[...] - me * PTS
    inside = (local >= 0) & (local < PTS)
    group_of = jnp.where(inside, local >> 7, -1)
    lane_of = local & (LANES - 1)
    for j in range(INDUCING // LANES):
        one_hot = jnp.where(lane_row == lane_of[j : j + 1], 1.0, 0.0).astype(jnp.bfloat16)
        picked = jnp.dot(stacked, one_hot, preferred_element_type=jnp.float32)
        which = jnp.broadcast_to(group_of[j : j + 1], (48, LANES))
        kept = jnp.zeros((48, LANES), jnp.float32)
        for g in range(8):
            kept = jnp.where(which == g, picked[g * 48 : (g + 1) * 48], kept)
        coords = kept[0:16] + kept[16:32] + kept[32:48]
        a_send[j] = coords[0:8]
        a_send[16 + j] = coords[8:16]

    pl.semaphore_wait(barrier, GROUP - 1 + PLANES - 1)

    a1 = scatter(0, a_send, a_recv)
    x1 = scatter(1, x_send, x_recv)
    get_w.wait()

    @pl.loop(1, 8)
    def _(k):
        pltpu.make_async_remote_copy(
            src_ref=w_all.at[col_id],
            dst_ref=w_all.at[col_id],
            send_sem=send_sem.at[2],
            recv_sem=recv_sem.at[2],
            device_id=(row_id, (col_id + k) % 8),
            device_id_type=MESH,
        ).start()

    w1 = arrival(2, w_all, 7, (row_id, (col_id + 1) % 8))

    owners = [order_ref[s] for s in range(STEPS)]
    owner_spot = [o & (GROUP - 1) for o in owners]
    owner_z = [o >> 5 for o in owners]

    a1.wait_recv()
    a_mid[z] = jnp.sum(a_recv[...], axis=0)
    a2 = along_z(3, a_mid)
    x1.wait_recv()
    for s in range(STEPS):
        x_mid[z, s] = x_recv[owner_spot[s]]
    x2 = along_z(4, x_mid)
    a2.wait_recv()
    a_all[spot] = jnp.sum(a_mid[...], axis=0)
    a3 = in_plane(5, a_all)
    x2.wait_recv()
    for s in range(STEPS):
        x_all[spot, s] = x_mid[owner_z[s], s]
    a3.wait_recv()
    x3 = in_plane(6, x_all)

    w1.wait_recv()
    get_targets.wait()

    warm = jnp.zeros((COLS, PTS), jnp.float32)
    for i in range(INDUCING // 256):
        coords = jnp.concatenate(
            [
                jnp.concatenate([a_all[2 * i], a_all[2 * i + 1]], axis=1),
                jnp.concatenate([a_all[16 + 2 * i], a_all[16 + 2 * i + 1]], axis=1),
            ],
            axis=0,
        )
        left = left_rows(*split3(coords), coords)
        warm += jnp.dot(
            w_all[i], tile_of(left, right[...]), preferred_element_type=jnp.float32
        )
    res_ref[...] -= warm

    wts_ref[...] = jnp.zeros_like(wts_ref)
    get_inverse.wait()

    def block_tile(s):
        @pl.loop(0, 4)
        def _(i):
            planes = [
                jnp.concatenate(
                    [x_all[p * 8 + 2 * i, s], x_all[p * 8 + 2 * i + 1, s]], axis=1
                )
                for p in range(3)
            ]
            coords = sum(p.astype(jnp.float32) for p in planes)
            left = left_rows(*planes, coords)
            ktile[s, pl.ds(pl.multiple_of(i * 256, 256), 256), :] = tile_of(left, right[...])

    for s in range(STEPS):
        shifted = res_ref[...].astype(jnp.bfloat16)
        for g in range(4):
            part = jnp.dot(
                shifted,
                inverse[:, g * 256 : (g + 1) * 256],
                preferred_element_type=jnp.float32,
            ).astype(jnp.bfloat16)
            for r in range(4):
                for h in range(2):
                    cand[s, r * 8 + g * 2 + h] = part[
                        r * 16 : (r + 1) * 16, h * LANES : (h + 1) * LANES
                    ]
        d1 = scatter(7 + 3 * s, cand.at[s], d_recv[s])
        if s == 0:
            x3.wait_recv()
            block_tile(0)
        d1.wait_recv()
        d_mid[s][z] = d_recv[s][owner_spot[s]]
        d2 = along_z(8 + 3 * s, d_mid[s])
        if s < STEPS - 1:
            block_tile(s + 1)
        d2.wait_recv()
        d_all[s, spot] = d_mid[s][owner_z[s]]
        d3 = in_plane(9 + 3 * s, d_all.at[s])
        d3.wait_recv()
        delta = jnp.concatenate(
            [
                jnp.concatenate([d_all[s, r * 8 + g] for g in range(8)], axis=1)
                for r in range(4)
            ],
            axis=0,
        )
        mine = (owners[s] == me).astype(jnp.float32)
        delta_f = delta.astype(jnp.float32) * mine
        update = jnp.dot(delta, ktile[s], preferred_element_type=jnp.float32)
        res_ref[...] = (res_ref[...] - update) - noise_var * delta_f
        wts_ref[...] += delta_f

    for transfer in pending:
        transfer.wait_send()


def projected(points, lengthscales, targets, inducing_weights, inducing_index, block_order, block_inverse):
    vmem = pl.BlockSpec(memory_space=pltpu.VMEM)
    hbm = pl.BlockSpec(memory_space=pltpu.HBM)
    out = jax.ShapeDtypeStruct((COLS, PTS), jnp.float32)
    bf16, f32 = jnp.bfloat16, jnp.float32
    return pl.pallas_call(
        body,
        out_shape=(out, out),
        in_specs=[hbm] * 7,
        out_specs=(vmem, vmem),
        scratch_shapes=[
            pltpu.VMEM((DIM, PTS), f32),
            pltpu.SMEM((DIM,), f32),
            pltpu.VMEM((INDUCING // LANES, LANES), jnp.int32),
            pltpu.SMEM((STEPS,), jnp.int32),
            pltpu.VMEM((PTS, PTS), bf16),
            pltpu.VMEM((8, COLS, 256), bf16),
            pltpu.VMEM((LANES, PTS), bf16),
            pltpu.VMEM((GROUP, 8, LANES), f32),
            pltpu.VMEM((GROUP, 8, LANES), f32),
            pltpu.VMEM((PLANES, 8, LANES), f32),
            pltpu.VMEM((GROUP, 8, LANES), f32),
            pltpu.VMEM((GROUP, 16, LANES), bf16),
            pltpu.VMEM((GROUP, 16, LANES), bf16),
            pltpu.VMEM((PLANES, STEPS, 16, LANES), bf16),
            pltpu.VMEM((GROUP, STEPS, 16, LANES), bf16),
            pltpu.VMEM((STEPS, GROUP, 16, LANES), bf16),
            *[pltpu.VMEM((GROUP, 16, LANES), bf16)] * STEPS,
            *[pltpu.VMEM((PLANES, 16, LANES), bf16)] * STEPS,
            pltpu.VMEM((STEPS, GROUP, 16, LANES), bf16),
            pltpu.VMEM((STEPS, PTS, PTS), bf16),
            pltpu.SemaphoreType.DMA((7,)),
            pltpu.SemaphoreType.DMA((16,)),
            pltpu.SemaphoreType.DMA((16,)),
        ],
        compiler_params=pltpu.CompilerParams(
            collective_id=0, has_side_effects=True, vmem_limit_bytes=62 << 20
        ),
        name="projection",
    )(
        points,
        lengthscales,
        targets,
        inducing_weights,
        inducing_index.reshape(INDUCING // LANES, LANES),
        block_order,
        block_inverse,
    )


def solution(mesh):
    placed = (
        P(None, ("rows", "cols")),
        P(),
        P(None, ("rows", "cols")),
        P(None, "cols"),
        P(),
        P(),
        P(("rows", "cols"), None, None),
    )
    return jax.shard_map(
        projected,
        mesh=mesh,
        in_specs=placed,
        out_specs=(P(None, ("rows", "cols")), P(None, ("rows", "cols"))),
        check_vma=False,
    )
```

```python
import functools
import math

import jax
import jax.numpy as jnp
from jax import lax
from jax.experimental import pallas as pl
from jax.experimental.pallas import tpu as pltpu
from jax.sharding import PartitionSpec as P

MESH = pl.DeviceIdType.MESH
noise_var = 0.5
LOG2E = math.log2(math.e)

DIM = 16
COLS = 64
PTS = 1024
STEPS = 3
PLANES = 8
GROUP = 32
INDUCING = 2048
LANES = 128


PLANE_ORDER = sorted(
    [(dx, dy, dc) for dx in range(4) for dy in range(4) for dc in range(2) if dx or dy or dc],
    key=lambda o: (-(min(o[0], 4 - o[0]) + min(o[1], 4 - o[1])), o[0] % 2, o[2], o[0], o[1]),
)
PLANE_STEPS = (4, 3, 5, 2, 6, 1, 7)


def split3(x):
    high = x.astype(jnp.bfloat16)
    rest = x - high.astype(jnp.float32)
    mid = rest.astype(jnp.bfloat16)
    low = (rest - mid.astype(jnp.float32)).astype(jnp.bfloat16)
    return high, mid, low


def norm_rows(norm, first):
    parts = [p.astype(jnp.float32) for p in split3(norm)]
    row = lax.broadcasted_iota(jnp.int32, (16, norm.shape[1]), 0)
    one_from = 3 - first
    out = jnp.where((row >= one_from) & (row < one_from + 3), 1.0, 0.0)
    for k in range(3):
        out = jnp.where(row == first + k, parts[k], out)
    return out.astype(jnp.bfloat16)


def left_rows(high, mid, low, x):
    norm = (-0.5 * LOG2E) * jnp.sum(x * x, axis=0, keepdims=True)
    rows = norm_rows(norm, 0)
    return jnp.concatenate([high, high, mid, high, low, mid, rows, jnp.zeros_like(rows)], axis=0)


def right_rows(x):
    norm = (-0.5 * LOG2E) * jnp.sum(x * x, axis=0, keepdims=True)
    high, mid, low = split3(x * LOG2E)
    rows = norm_rows(norm, 3)
    return jnp.concatenate([high, mid, high, low, high, mid, rows, jnp.zeros_like(rows)], axis=0)


def tile_of(left, right):
    power = lax.dot_general(
        left, right, (((0,), (0,)), ((), ())), preferred_element_type=jnp.float32
    )
    return jnp.exp2(power).astype(jnp.bfloat16)


def body(
    pts_hbm,
    scale_hbm,
    targets_ref,
    own_w_ref,
    index_hbm,
    order_hbm,
    inverse_ref,
    res_ref,
    wts_ref,
    pts_ref,
    scale_ref,
    index_ref,
    order_ref,
    inverse,
    w_all,
    right,
    a_send,
    a_recv,
    a_mid,
    a_all,
    x_send,
    x_recv,
    x_mid,
    x_all,
    cand,
    d_recv0,
    d_recv1,
    d_recv2,
    d_mid0,
    d_mid1,
    d_mid2,
    d_all,
    ktile,
    local_sem,
    send_sem,
    recv_sem,
):
    d_recv = (d_recv0, d_recv1, d_recv2)
    d_mid = (d_mid0, d_mid1, d_mid2)
    row_id = lax.axis_index("rows")
    col_id = lax.axis_index("cols")
    z = row_id // 4
    spot = (row_id % 4) * 8 + col_id
    me = row_id * 8 + col_id

    x_pos, y_pos, core = row_id % 4, col_id // 2, col_id % 2
    xs = [x_pos] + [(x_pos + d) % 4 for d in (1, 2, 3)]
    ys = [y_pos] + [(y_pos + d) % 4 for d in (1, 2, 3)]
    cores = (core, 1 - core)
    others = []
    for dx, dy, dc in PLANE_ORDER:
        others.append(
            (
                xs[dx] * 8 + ys[dy] * 2 + cores[dc],
                (z * 4 + xs[dx], ys[dy] * 2 + cores[dc]),
            )
        )
    planes = [(((z + k) % PLANES) * 4 + x_pos, col_id) for k in PLANE_STEPS]

    barrier = pltpu.get_barrier_semaphore()
    for _, place in others:
        pl.semaphore_signal(barrier, inc=1, device_id=place, device_id_type=MESH)
    for place in planes:
        pl.semaphore_signal(barrier, inc=1, device_id=place, device_id_type=MESH)

    get_inverse = pltpu.make_async_copy(inverse_ref.at[0], inverse, local_sem.at[0])
    get_targets = pltpu.make_async_copy(targets_ref, res_ref, local_sem.at[1])
    get_w = pltpu.make_async_copy(own_w_ref, w_all.at[col_id], local_sem.at[2])
    small = [
        pltpu.make_async_copy(src, dst, local_sem.at[3 + k])
        for k, (src, dst) in enumerate(
            [
                (pts_hbm, pts_ref),
                (scale_hbm, scale_ref),
                (index_hbm, index_ref),
                (order_hbm, order_ref),
            ]
        )
    ]
    for copy in small:
        copy.start()
    get_w.start()
    get_targets.start()
    get_inverse.start()

    pending = []

    def send(phase, src, dst, place):
        pltpu.make_async_remote_copy(
            src_ref=src,
            dst_ref=dst,
            send_sem=send_sem.at[phase],
            recv_sem=recv_sem.at[phase],
            device_id=place,
            device_id_type=MESH,
        ).start()

    def arrival(phase, dst, count, other):
        some = dst.at[pl.ds(0, count)]
        all_of_them = pltpu.make_async_remote_copy(
            src_ref=some,
            dst_ref=some,
            send_sem=send_sem.at[phase],
            recv_sem=recv_sem.at[phase],
            device_id=other,
            device_id_type=MESH,
        )
        pending.append(all_of_them)
        return all_of_them

    def scatter(phase, src, dst):
        for there, place in others:
            send(phase, src.at[there], dst.at[spot], place)
        dst[spot] = src[spot]
        return arrival(phase, dst, GROUP - 1, others[0][1])

    def along_z(phase, dst):
        for place in planes:
            send(phase, dst.at[z], dst.at[z], place)
        return arrival(phase, dst, PLANES - 1, planes[0])

    def in_plane(phase, dst):
        for _, place in others:
            send(phase, dst.at[spot], dst.at[spot], place)
        return arrival(phase, dst, GROUP - 1, others[0][1])

    for copy in small:
        copy.wait()
    feature = lax.broadcasted_iota(jnp.int32, (DIM, PTS), 0)
    scales = jnp.zeros((DIM, PTS), jnp.float32)
    for k in range(DIM):
        scales = jnp.where(feature == k, scale_ref[k], scales)
    scaled = pts_ref[...] / scales
    right[...] = right_rows(scaled)
    parts = split3(scaled)
    for p in range(3):
        for g in range(8):
            x_send[p * 8 + g] = parts[p][:, g * LANES : (g + 1) * LANES]
    x_send[pl.ds(24, 8)] = jnp.zeros((8, 16, LANES), jnp.bfloat16)
    stacked = jnp.concatenate(
        [parts[p][:, g * LANES : (g + 1) * LANES] for g in range(8) for p in range(3)], axis=0
    )
    lane_row = lax.broadcasted_iota(jnp.int32, (LANES, LANES), 0)
    local = index_ref[...] - me * PTS
    inside = (local >= 0) & (local < PTS)
    group_of = jnp.where(inside, local >> 7, -1)
    lane_of = local & (LANES - 1)
    for j in range(INDUCING // LANES):
        one_hot = jnp.where(lane_row == lane_of[j : j + 1], 1.0, 0.0).astype(jnp.bfloat16)
        picked = jnp.dot(stacked, one_hot, preferred_element_type=jnp.float32)
        which = jnp.broadcast_to(group_of[j : j + 1], (48, LANES))
        kept = jnp.zeros((48, LANES), jnp.float32)
        for g in range(8):
            kept = jnp.where(which == g, picked[g * 48 : (g + 1) * 48], kept)
        coords = kept[0:16] + kept[16:32] + kept[32:48]
        a_send[j] = coords[0:8]
        a_send[16 + j] = coords[8:16]

    pl.semaphore_wait(barrier, GROUP - 1 + PLANES - 1)

    a1 = scatter(0, a_send, a_recv)
    get_w.wait()
    siblings = [o for o, (dx, _, _) in zip(others, PLANE_ORDER) if dx == 0]
    for _, place in siblings[:3]:
        send(2, w_all.at[col_id], w_all.at[col_id], place)

    owners = [order_ref[s] for s in range(STEPS)]
    owner_spot = [o & (GROUP - 1) for o in owners]
    owner_z = [o >> 5 for o in owners]

    a1.wait_recv()
    a_mid[z] = jnp.sum(a_recv[...], axis=0)
    a2 = along_z(3, a_mid)
    for _, place in siblings[3:]:
        send(2, w_all.at[col_id], w_all.at[col_id], place)
    w1 = arrival(2, w_all, 7, siblings[0][1])
    x1 = scatter(1, x_send, x_recv)
    a2.wait_recv()
    a_all[spot] = jnp.sum(a_mid[...], axis=0)
    a3 = in_plane(5, a_all)
    x1.wait_recv()
    for s in range(STEPS):
        x_mid[z, s] = x_recv[owner_spot[s]]
    x2 = along_z(4, x_mid)
    a3.wait_recv()

    w1.wait_recv()
    get_targets.wait()

    warm = jnp.zeros((COLS, PTS), jnp.float32)
    for i in range(INDUCING // 256):
        coords = jnp.concatenate(
            [
                jnp.concatenate([a_all[2 * i], a_all[2 * i + 1]], axis=1),
                jnp.concatenate([a_all[16 + 2 * i], a_all[16 + 2 * i + 1]], axis=1),
            ],
            axis=0,
        )
        left = left_rows(*split3(coords), coords)
        warm += jnp.dot(
            w_all[i], tile_of(left, right[...]), preferred_element_type=jnp.float32
        )
    res_ref[...] -= warm

    wts_ref[...] = jnp.zeros_like(wts_ref)
    get_inverse.wait()

    def block_tile(s):
        for i in range(4):
            planes_of = [
                jnp.concatenate(
                    [x_all[s, p * 8 + 2 * i], x_all[s, p * 8 + 2 * i + 1]], axis=1
                )
                for p in range(3)
            ]
            coords = sum(p.astype(jnp.float32) for p in planes_of)
            left = left_rows(*planes_of, coords)
            ktile[i * 256 : (i + 1) * 256, :] = tile_of(left, right[...])

    for s in range(STEPS):
        shifted = res_ref[...].astype(jnp.bfloat16)
        for g in range(4):
            part = jnp.dot(
                shifted,
                inverse[:, g * 256 : (g + 1) * 256],
                preferred_element_type=jnp.float32,
            ).astype(jnp.bfloat16)
            for r in range(4):
                for h in range(2):
                    cand[s, r * 8 + g * 2 + h] = part[
                        r * 16 : (r + 1) * 16, h * LANES : (h + 1) * LANES
                    ]
        d1 = scatter(7 + 4 * s, cand.at[s], d_recv[s])
        if s == 0:
            x2.wait_recv()
        d1.wait_recv()
        d_mid[s][z] = d_recv[s][owner_spot[s]]
        d2 = along_z(8 + 4 * s, d_mid[s])
        x_all[s, spot] = x_mid[owner_z[s], s]
        x3 = in_plane(10 + 4 * s, x_all.at[s])
        d2.wait_recv()
        d_all[s, spot] = d_mid[s][owner_z[s]]
        d3 = in_plane(9 + 4 * s, d_all.at[s])
        x3.wait_recv()
        block_tile(s)
        d3.wait_recv()
        delta = jnp.concatenate(
            [
                jnp.concatenate([d_all[s, r * 8 + g] for g in range(8)], axis=1)
                for r in range(4)
            ],
            axis=0,
        )
        mine = (owners[s] == me).astype(jnp.float32)
        delta_f = delta.astype(jnp.float32) * mine
        update = jnp.dot(delta, ktile[...], preferred_element_type=jnp.float32)
        res_ref[...] = (res_ref[...] - update) - noise_var * delta_f
        wts_ref[...] += delta_f

    for transfer in pending:
        transfer.wait_send()


def projected(points, lengthscales, targets, inducing_weights, inducing_index, block_order, block_inverse):
    vmem = pl.BlockSpec(memory_space=pltpu.VMEM)
    hbm = pl.BlockSpec(memory_space=pltpu.HBM)
    out = pltpu.VMEM((COLS, PTS), jnp.float32)
    bf16, f32 = jnp.bfloat16, jnp.float32
    return pl.pallas_call(
        body,
        out_shape=(out, out),
        in_specs=[hbm] * 7,
        out_specs=(vmem, vmem),
        scratch_shapes=[
            pltpu.VMEM((DIM, PTS), f32),
            pltpu.SMEM((DIM,), f32),
            pltpu.VMEM((INDUCING // LANES, LANES), jnp.int32),
            pltpu.SMEM((STEPS,), jnp.int32),
            pltpu.VMEM((PTS, PTS), bf16),
            pltpu.VMEM((8, COLS, 256), bf16),
            pltpu.VMEM((LANES, PTS), bf16),
            pltpu.VMEM((GROUP, 8, LANES), f32),
            pltpu.VMEM((GROUP, 8, LANES), f32),
            pltpu.VMEM((PLANES, 8, LANES), f32),
            pltpu.VMEM((GROUP, 8, LANES), f32),
            pltpu.VMEM((GROUP, 16, LANES), bf16),
            pltpu.VMEM((GROUP, 16, LANES), bf16),
            pltpu.VMEM((PLANES, STEPS, 16, LANES), bf16),
            pltpu.VMEM((STEPS, GROUP, 16, LANES), bf16),
            pltpu.VMEM((STEPS, GROUP, 16, LANES), bf16),
            *[pltpu.VMEM((GROUP, 16, LANES), bf16)] * STEPS,
            *[pltpu.VMEM((PLANES, 16, LANES), bf16)] * STEPS,
            pltpu.VMEM((STEPS, GROUP, 16, LANES), bf16),
            pltpu.VMEM((PTS, PTS), bf16),
            pltpu.SemaphoreType.DMA((7,)),
            pltpu.SemaphoreType.DMA((19,)),
            pltpu.SemaphoreType.DMA((19,)),
        ],
        compiler_params=pltpu.CompilerParams(
            collective_id=0, has_side_effects=True, vmem_limit_bytes=62 << 20
        ),
        name="projection",
    )(
        points,
        lengthscales,
        targets,
        inducing_weights,
        inducing_index.reshape(INDUCING // LANES, LANES),
        block_order,
        block_inverse,
    )


def solution(mesh):
    placed = (
        P(None, ("rows", "cols")),
        P(),
        P(None, ("rows", "cols")),
        P(None, "cols"),
        P(),
        P(),
        P(("rows", "cols"), None, None),
    )
    return jax.shard_map(
        projected,
        mesh=mesh,
        in_specs=placed,
        out_specs=(P(None, ("rows", "cols")), P(None, ("rows", "cols"))),
        check_vma=False,
    )
```
